32 devices in a mesh: samp: 8 (over z, x), blk: 4 (over y, core).
Axes of the slice: x: 2, y: 2, z: 4, core: 2. Of those that a mesh axis runs over, the one named last changes fastest.
Arguments:
- dosages: int32 [12288, 2048], P('samp', 'blk'), may hold values from 0 to 2, as said below
- new_dosages: int32 [12288, 512], P('samp', 'blk'), may hold values from 0 to 2, as said below
- traits: float32 [64, 12288], P(None, 'samp'), may hold values from -40 to 40
- shrink: float32 [5], replicated, may hold values from 0.5 to 5
Outputs:
- residual: float32 [5, 64, 12288], P(None, 'blk', 'samp')
- scores: float32 [5, 64, 512], P(None, None, 'blk')
The draws below stay inside these ranges and needn't reach their ends.
Inputs may be any that keep to these rules, and one draw needn't show every extreme that they name: `dosages`: codes of haplotype pairs, with linkage along neighbouring variants. `new_dosages`: codes of haplotype pairs, with linkage along neighbouring variants.
All inputs are finite; a program needn't handle non-finite values.
Results may differ from the reference program's by a relative error of at most 0.0053.
Values may be sent and summed in bfloat16 or wider, within the bound.
A program may use at most 64 MiB of HBM per device.

```python
import math
import jax
import jax.numpy as jnp
from jax import lax

VB = 512
TRAITS = 64
RIDGE = 5
CHEB = 3
SAMPLES = 12288
BLOCKS = 4
VARIANTS = 2048
NEW_TOTAL = 512


def haplotype_codes(base_key, row_count, column_count):
    level_key, column_key, start_key = jax.random.split(base_key, 3)
    allele_levels = jax.random.randint(level_key, (column_count,), 1, 8)
    column_keys = jax.random.split(column_key, column_count)
    bit_shape = (2 * row_count,)
    start_bits = jax.random.randint(start_key, bit_shape, 0, 2)

    def advance(previous, scan_inputs):
        one_key, allele_level = scan_inputs
        copy_key, fresh_key = jax.random.split(one_key)
        copy_mask = jax.random.randint(copy_key, bit_shape, 0, 4) < 3
        fresh_bits = (jax.random.randint(fresh_key, bit_shape, 0, 8) < allele_level).astype(jnp.int32)
        current = jnp.where(copy_mask, previous, fresh_bits)
        return (current, current)
    unused, haplotypes = lax.scan(advance, start_bits, (column_keys, allele_levels))
    code_matrix = haplotypes[:, :row_count] + haplotypes[:, row_count:]
    return code_matrix.T.astype(jnp.int32)


def draw_dosages(key, part):
    return haplotype_codes(jax.random.fold_in(key, 11), SAMPLES, VARIANTS)


def draw_new_dosages(key, part):
    return haplotype_codes(jax.random.fold_in(key, 12), SAMPLES, NEW_TOTAL)


def draw_traits(key, part):
    code_matrix = haplotype_codes(jax.random.fold_in(key, 11), SAMPLES, VARIANTS)
    effect = jax.random.normal(jax.random.fold_in(key, 13), (VARIANTS, TRAITS), jnp.float32)
    effect = effect * jnp.sqrt(0.5 / (2.6 * VARIANTS))
    genetic = jnp.dot(code_matrix.astype(jnp.float32) - 1.0, effect)
    noise_key = jax.random.fold_in(key, 14)
    noise = 0.7 * jax.random.truncated_normal(noise_key, -4.0, 4.0, (SAMPLES, TRAITS), jnp.float32)
    trait_scale = jnp.ones((TRAITS,), jnp.float32)
    values = (genetic + noise) * trait_scale[None, :]
    return jnp.clip(values, -40.0, 40.0).T


def setup_inputs(seed: int = 0) -> dict:
    streams_of = jax.random.split(jax.random.key(seed), 5)
    return {
        "dosages": draw_dosages(jax.random.fold_in(streams_of[4], 71), 0),
        "new_dosages": draw_new_dosages(jax.random.fold_in(streams_of[4], 71), 0),
        "traits": draw_traits(jax.random.fold_in(streams_of[4], 71), 0),
        "shrink": jnp.clip(jnp.exp(jax.random.uniform(streams_of[3], (RIDGE,), jnp.float32, math.log(0.5), math.log(5.0))), 0.5, 5.0),
    }


def standardize(code_block, count):
    values = code_block.astype(jnp.float32)
    column_mean = lax.optimization_barrier(jnp.sum(values, axis=0)) / count
    column_var = lax.optimization_barrier(jnp.sum(values * values, axis=0)) / count - column_mean * column_mean
    inverse = 1.0 / jnp.sqrt(column_var + 1e-05)
    return ((values - column_mean) * inverse).astype(jnp.bfloat16)

def chebyshev(rhs_cols, apply_fn, centre, half_width, sweeps):
    sig_ratio = centre / half_width
    factor = 1.0 / sig_ratio
    direction = rhs_cols / centre
    iterate = jnp.zeros_like(rhs_cols)
    remain = rhs_cols
    for sweep_index in range(sweeps):
        iterate = iterate + direction
        if sweep_index + 1 < sweeps:
            remain = remain - apply_fn(direction)
            factor_next = 1.0 / (2.0 * sig_ratio - factor)
            direction = factor_next * factor * direction + 2.0 * factor_next / half_width * remain
            factor = factor_next
    return iterate

def reference(dosages, new_dosages, traits, shrink):
    count = float(dosages.shape[0])
    trait_bf = traits.astype(jnp.bfloat16)
    lam_cols = jnp.repeat(shrink, TRAITS)

    def block_term(total, block_id):
        codes = lax.dynamic_slice_in_dim(dosages, block_id * VB, VB, 1)
        standard = standardize(codes, count)
        gram = jnp.dot(standard.T, standard, preferred_element_type=jnp.float32)
        cross = jnp.dot(standard.T, trait_bf.T, preferred_element_type=jnp.float32)
        bound = jnp.max(lax.optimization_barrier(jnp.sum(jnp.abs(gram), axis=0))) / count
        rhs_cols = jnp.tile(cross / count, (1, RIDGE))

        def apply_fn(direction):
            return jnp.dot(gram, direction, precision=lax.Precision.HIGHEST) / count + lam_cols * direction
        centre = lam_cols + bound / 2.0
        half_width = bound / 2.0 + jnp.zeros_like(lam_cols)
        weights = chebyshev(rhs_cols, apply_fn, centre, half_width, CHEB).astype(jnp.bfloat16)
        pred = jnp.dot(weights.T, standard.T, preferred_element_type=jnp.float32)
        return (total + pred, None)
    start_total = jnp.zeros((RIDGE * TRAITS, dosages.shape[0]), jnp.float32)
    pred, unused = lax.scan(block_term, start_total, jnp.arange(BLOCKS, dtype=jnp.int32))
    residual = traits[None, :, :] - pred.reshape(RIDGE, TRAITS, dosages.shape[0])
    res_bf = residual.astype(jnp.bfloat16).reshape(RIDGE * TRAITS, dosages.shape[0])
    fresh = standardize(new_dosages, count)
    raw = jnp.dot(res_bf, fresh, preferred_element_type=jnp.float32)
    res_float = res_bf.astype(jnp.float32)
    sum_sq = lax.optimization_barrier(jnp.sum(res_float * res_float, axis=1))
    scores = raw / jnp.sqrt(count * (sum_sq / count + 1e-05))[:, None]
    return (residual, scores.reshape(RIDGE, TRAITS, new_dosages.shape[1]))
```

```python
import functools

import jax
import jax.numpy as jnp
from jax import lax
from jax.experimental import pallas as pl
from jax.experimental.pallas import tpu as pltpu
from jax.sharding import PartitionSpec as P

RIDGE = 5
CHEB = 3
LANES = 128
F32 = jnp.float32
BF16 = jnp.bfloat16
MESH = pl.DeviceIdType.MESH


def up(value, unit):
    return -(-value // unit) * unit


def coefficients(lam, bound):
    centre = lam + bound / 2.0
    half = bound / 2.0
    sig = centre / half
    factor = 1.0 / sig
    zero = jnp.zeros_like(centre)
    direction = [1.0 / centre] + [zero] * (CHEB - 1)
    remain = [zero + 1.0] + [zero] * (CHEB - 1)
    iterate = [zero] * CHEB
    for sweep in range(CHEB):
        iterate = [a + b for a, b in zip(iterate, direction)]
        if sweep + 1 < CHEB:
            applied = [lam * direction[0]] + [
                lam * direction[i] + direction[i - 1] for i in range(1, CHEB)
            ]
            remain = [a - b for a, b in zip(remain, applied)]
            following = 1.0 / (2.0 * sig - factor)
            direction = [
                following * factor * a + 2.0 * following / half * b
                for a, b in zip(direction, remain)
            ]
            factor = following
    return iterate


def kernel(
    ns, nb, share, count, chunk,
    shrink_ref, dos_ref, new_ref, traits_ref,
    residual_ref, scores_ref,
    x_ref, fresh_ref, st_src, st_dst, part, rs_dst, gath, gram_ref, w_ref,
    core_src, keep, core_dst, y_src, y_dst, rw_src, rw_dst, fin_src, fin_dst,
    st_s, st_r, rs_s, rs_r, ag_s, ag_r, fr_s, fr_r, core_s, core_r, y_s, y_r,
    rw_s, rw_r, fin_s, fin_r,
):
    s = lax.axis_index("samp")
    b = lax.axis_index("blk")
    ny = nb // 2
    core = lax.rem(b, 2)
    y = b // 2
    rows, vb = dos_ref.shape
    nc = new_ref.shape[1]
    nt = traits_ref.shape[0]
    vblocks = vb // LANES
    own = RIDGE * share
    q = nb * own // ns
    k = ns // nb
    total = ns * nb
    me = s * nb + b

    barrier = pltpu.get_barrier_semaphore()

    def greet(i, carry):
        other = lax.rem(me + i, total)
        pl.semaphore_signal(
            barrier, inc=1, device_id=(other // nb, lax.rem(other, nb)), device_id_type=MESH
        )
        return carry

    lax.fori_loop(1, total, greet, 0)

    sends = []

    def send(src, dst, ssem, rsem, device):
        copy = pltpu.make_async_remote_copy(
            src_ref=src, dst_ref=dst, send_sem=ssem, recv_sem=rsem,
            device_id=device, device_id_type=MESH,
        )
        copy.start()
        sends.append(copy)
        return copy

    st_src[...] = jnp.zeros_like(st_src)
    codes = dos_ref[...].astype(F32)
    st_src[0:1, :vb] = jnp.sum(codes, axis=0, keepdims=True)
    st_src[1:2, :vb] = jnp.sum(codes * codes, axis=0, keepdims=True)
    codes = new_ref[...].astype(F32)
    st_src[0:1, vb:] = jnp.sum(codes, axis=0, keepdims=True)
    st_src[1:2, vb:] = jnp.sum(codes * codes, axis=0, keepdims=True)

    pl.semaphore_wait(barrier, total - 1)
    copies = []
    for o in range(1, ns):
        copies.append(
            send(st_src, st_dst.at[o], st_s.at[o], st_r.at[o], (lax.rem(s + o, ns), b))
        )
    stat = st_src[...]
    for o in range(1, ns):
        copies[o - 1].wait_recv()
        stat = stat + st_dst[o]
    mean = stat[0:1] / count
    inv = 1.0 / jnp.sqrt(stat[1:2] / count - mean * mean + 1e-05)
    fresh_ref[b] = ((new_ref[...].astype(F32) - mean[:, vb:]) * inv[:, vb:]).astype(BF16)
    fresh_copies = []
    for o in range(1, nb):
        fresh_copies.append(
            send(fresh_ref.at[b], fresh_ref.at[b], fr_s.at[o], fr_r.at[o], (s, lax.rem(b + o, nb)))
        )
    x_ref[...] = ((dos_ref[...].astype(F32) - mean[:, :vb]) * inv[:, :vb]).astype(BF16)

    x = x_ref[...]
    at = 0
    for i in range(vblocks):
        line = lax.dot_general(
            x[:, i * LANES : (i + 1) * LANES], x[:, i * LANES :],
            (((0,), (0,)), ((), ())), preferred_element_type=F32,
        ).astype(BF16)
        for j in range(vblocks - i):
            part[at : at + LANES, :] = line[:, j * LANES : (j + 1) * LANES]
            at += LANES
    cross = jnp.dot(
        traits_ref[...].astype(BF16), x, preferred_element_type=F32
    ).astype(BF16)
    for j in range(vblocks):
        part[at : at + nt, :] = cross[:, j * LANES : (j + 1) * LANES]
        at += nt
    if at < ns * chunk:
        part[at:, :] = jnp.zeros((ns * chunk - at, LANES), BF16)

    def piece(index):
        return pl.ds(pl.multiple_of(index * chunk, 16), chunk)

    copies = []
    for o in range(1, ns):
        to = lax.rem(s + o, ns)
        copies.append(
            send(part.at[piece(to)], rs_dst.at[o], rs_s.at[o], rs_r.at[o], (to, b))
        )
    summed = part[piece(s), :].astype(F32)
    for o in range(1, ns):
        copies[o - 1].wait_recv()
        summed = summed + rs_dst[o].astype(F32)
    gath[piece(s), :] = summed.astype(BF16)
    copies = []
    for o in range(1, ns):
        to = lax.rem(s + o, ns)
        copies.append(
            send(gath.at[piece(s)], gath.at[piece(s)], ag_s.at[o], ag_r.at[o], (to, b))
        )
    for o in range(1, ns):
        source = lax.rem(s - o + ns, ns)
        pltpu.make_async_remote_copy(
            src_ref=gath.at[piece(source)], dst_ref=gath.at[piece(source)],
            send_sem=ag_s.at[o], recv_sem=ag_r.at[o],
            device_id=(source, b), device_id_type=MESH,
        ).wait_recv()

    at = 0
    for i in range(vblocks):
        for j in range(i, vblocks):
            block = gath[at : at + LANES, :].astype(F32)
            at += LANES
            gram_ref[i * LANES : (i + 1) * LANES, j * LANES : (j + 1) * LANES] = block.astype(BF16)
            if j > i:
                gram_ref[j * LANES : (j + 1) * LANES, i * LANES : (i + 1) * LANES] = block.T.astype(BF16)
    cross = jnp.concatenate(
        [gath[at + j * nt : at + (j + 1) * nt, :] for j in range(vblocks)], axis=1
    )
    gram = gram_ref[...]
    bound = jnp.max(
        jnp.sum(jnp.abs(gram.astype(F32)), axis=0, keepdims=True), axis=1, keepdims=True
    ) / count
    bound = jnp.broadcast_to(bound, (1, vb))

    def apply(value):
        high = value.astype(BF16)
        low = (value - high.astype(F32)).astype(BF16)
        return (
            jnp.dot(high, gram, preferred_element_type=F32)
            + jnp.dot(low, gram, preferred_element_type=F32)
        ) / count

    powers = [cross.astype(F32) / count]
    for _ in range(CHEB - 1):
        powers.append(apply(powers[-1]))
    for r in range(RIDGE):
        coefs = coefficients(jnp.full((1, vb), shrink_ref[r], F32), bound)
        weight = coefs[0] * powers[0]
        for c, v in zip(coefs[1:], powers[1:]):
            weight = weight + c * v
        weight = weight.astype(BF16)
        for d in range(nb):
            w_ref[d, r * share : (r + 1) * share, :] = weight[d * share : (d + 1) * share, :]

    for d in range(nb):
        pred = lax.dot_general(
            w_ref[d], x, (((1,), (1,)), ((), ())), preferred_element_type=F32
        )

        @pl.when(core == d % 2)
        def _():
            keep[d // 2] = pred

        @pl.when(core != d % 2)
        def _():
            core_src[d // 2] = pred.astype(BF16)

    copy = send(core_src, core_dst, core_s.at[0], core_r.at[0], (s, 2 * y + 1 - core))
    copy.wait_recv()
    copies = []
    for o in range(1, ny):
        to = lax.rem(y + o, ny)
        y_src[o] = (keep[to] + core_dst[to].astype(F32)).astype(BF16)
        copies.append(
            send(y_src.at[o], y_dst.at[o], y_s.at[o], y_r.at[o], (s, 2 * to + core))
        )
    pred = keep[y] + core_dst[y].astype(F32)
    for o in range(1, ny):
        copies[o - 1].wait_recv()
        pred = pred + y_dst[o].astype(F32)
    mine = traits_ref[pl.ds(pl.multiple_of(b * share, 8), share), :]
    resid = jnp.concatenate([mine] * RIDGE, axis=0) - pred
    for r in range(RIDGE):
        residual_ref[r] = resid[r * share : (r + 1) * share, :]
    res_bf = resid.astype(BF16)
    res_f = res_bf.astype(F32)
    squares = jnp.zeros((own, LANES), F32)
    for j in range(rows // LANES):
        v = res_f[:, j * LANES : (j + 1) * LANES]
        squares = squares + v * v
    for copy in fresh_copies:
        copy.wait_recv()
    for d in range(nb):
        raw = jnp.dot(res_bf, fresh_ref[d], preferred_element_type=F32)
        for i in range(k):
            rw_src[d * k + i, 0] = raw[i * q : (i + 1) * q, :]
            rw_src[d * k + i, 1] = squares[i * q : (i + 1) * q, :]
    copies = []
    for o in range(1, ns):
        to = lax.rem(s + o, ns)
        copies.append(send(rw_src.at[to], rw_dst.at[o], rw_s.at[o], rw_r.at[o], (to, b)))
    raw = rw_src[s, 0]
    squares = rw_src[s, 1]
    for o in range(1, ns):
        copies[o - 1].wait_recv()
        raw = raw + rw_dst[o, 0]
        squares = squares + rw_dst[o, 1]
    norm = jnp.sum(squares, axis=1, keepdims=True)
    fin_src[...] = raw / jnp.sqrt(count * (norm / count + 1e-05))

    goal = s // k
    slot = lax.rem(s, k)
    for o in range(ns):
        copy = pltpu.make_async_remote_copy(
            src_ref=fin_src, dst_ref=fin_dst.at[b, slot],
            send_sem=fin_s.at[o], recv_sem=fin_r.at[slot * nb + b],
            device_id=(lax.rem(s + o, ns), goal), device_id_type=MESH,
        )
        if o == 0:
            @pl.when(goal != b)
            def _():
                copy.start()

            @pl.when(goal == b)
            def _():
                fin_dst[b, slot] = fin_src[...]
        else:
            copy.start()
            sends.append(copy)
    for i in range(k):
        for d in range(nb):
            source = b * k + i

            @pl.when(jnp.logical_or(source != s, b != d))
            def _():
                pltpu.make_async_remote_copy(
                    src_ref=fin_src, dst_ref=fin_dst.at[d, i],
                    send_sem=fin_s.at[0], recv_sem=fin_r.at[i * nb + d],
                    device_id=(source, d), device_id_type=MESH,
                ).wait_recv()

    for d in range(nb):
        block = jnp.concatenate([fin_dst[d, i] for i in range(k)], axis=0)
        for r in range(RIDGE):
            scores_ref[r, d * share : (d + 1) * share, :] = block[r * share : (r + 1) * share, :]

    for copy in sends:
        copy.wait_send()

    @pl.when(goal != b)
    def _():
        pltpu.make_async_remote_copy(
            src_ref=fin_src, dst_ref=fin_dst.at[b, slot],
            send_sem=fin_s.at[0], recv_sem=fin_r.at[slot * nb + b],
            device_id=(s, goal), device_id_type=MESH,
        ).wait_send()


def shards(ns, nb, dosages, new_dosages, traits, shrink):
    rows, vb = dosages.shape
    nc = new_dosages.shape[1]
    real = traits.shape[0] // nb
    share = up(real, 16)
    if share != real:
        traits = jnp.pad(
            traits.reshape(nb, real, rows), ((0, 0), (0, share - real), (0, 0))
        ).reshape(nb * share, rows)
    nt = nb * share
    vblocks = vb // LANES
    chunk = up(-(-(vblocks * (vblocks + 1) // 2 * LANES + vblocks * nt) // ns), 16)
    own = RIDGE * share
    ny = nb // 2
    k = ns // nb
    q = own // k
    count = float(rows * ns)
    dma = pltpu.SemaphoreType.DMA
    vmem = pl.BlockSpec(memory_space=pltpu.VMEM)
    residual, scores = pl.pallas_call(
        functools.partial(kernel, ns, nb, share, count, chunk),
        out_shape=(
            jax.ShapeDtypeStruct((RIDGE, share, rows), F32),
            jax.ShapeDtypeStruct((RIDGE, nt, nc), F32),
        ),
        in_specs=[pl.BlockSpec(memory_space=pltpu.SMEM), vmem, vmem, vmem],
        out_specs=(vmem, vmem),
        scratch_shapes=[
            pltpu.VMEM((rows, vb), BF16),
            pltpu.VMEM((nb, rows, nc), BF16),
            pltpu.VMEM((8, vb + nc), F32),
            pltpu.VMEM((ns, 8, vb + nc), F32),
            pltpu.VMEM((ns * chunk, LANES), BF16),
            pltpu.VMEM((ns, chunk, LANES), BF16),
            pltpu.VMEM((ns * chunk, LANES), BF16),
            pltpu.VMEM((vb, vb), BF16),
            pltpu.VMEM((nb, own, vb), BF16),
            pltpu.VMEM((ny, own, rows), BF16),
            pltpu.VMEM((ny, own, rows), F32),
            pltpu.VMEM((ny, own, rows), BF16),
            pltpu.VMEM((ny, own, rows), BF16),
            pltpu.VMEM((ny, own, rows), BF16),
            pltpu.VMEM((ns, 2, q, nc), F32),
            pltpu.VMEM((ns, 2, q, nc), F32),
            pltpu.VMEM((q, nc), F32),
            pltpu.VMEM((nb, k, q, nc), F32),
            dma((ns,)), dma((ns,)), dma((ns,)), dma((ns,)), dma((ns,)), dma((ns,)),
            dma((nb,)), dma((nb,)), dma((1,)), dma((1,)), dma((ny,)), dma((ny,)),
            dma((ns,)), dma((ns,)), dma((ns,)), dma((ns,)),
        ],
        compiler_params=pltpu.CompilerParams(
            collective_id=0, has_side_effects=True, vmem_limit_bytes=56 * 1024 * 1024
        ),
    )(shrink, dosages, new_dosages, traits)
    if share != real:
        residual = residual[:, :real]
        scores = scores.reshape(RIDGE, nb, share, nc)[:, :, :real].reshape(RIDGE, nb * real, nc)
    return residual, scores


def solution(mesh):
    placed = (P("samp", "blk"), P("samp", "blk"), P(None, "samp"), P())
    return jax.shard_map(
        functools.partial(shards, mesh.shape["samp"], mesh.shape["blk"]),
        mesh=mesh,
        in_specs=placed,
        out_specs=(P(None, "blk", "samp"), P(None, None, "blk")),
        check_vma=False,
    )
```

```python
import functools

import jax
import jax.numpy as jnp
from jax import lax
from jax.experimental import pallas as pl
from jax.experimental.pallas import tpu as pltpu
from jax.sharding import PartitionSpec as P

RIDGE = 5
CHEB = 3
LANES = 128
F32 = jnp.float32
BF16 = jnp.bfloat16
MESH = pl.DeviceIdType.MESH


def up(value, unit):
    return -(-value // unit) * unit


def coefficients(lam, bound):
    centre = lam + bound / 2.0
    half = bound / 2.0
    sig = centre / half
    factor = 1.0 / sig
    zero = jnp.zeros_like(centre)
    direction = [1.0 / centre] + [zero] * (CHEB - 1)
    remain = [zero + 1.0] + [zero] * (CHEB - 1)
    iterate = [zero] * CHEB
    for sweep in range(CHEB):
        iterate = [a + b for a, b in zip(iterate, direction)]
        if sweep + 1 < CHEB:
            applied = [lam * direction[0]] + [
                lam * direction[i] + direction[i - 1] for i in range(1, CHEB)
            ]
            remain = [a - b for a, b in zip(remain, applied)]
            following = 1.0 / (2.0 * sig - factor)
            direction = [
                following * factor * a + 2.0 * following / half * b
                for a, b in zip(direction, remain)
            ]
            factor = following
    return iterate


def kernel(
    ns, nb, share, count, chunk,
    shrink_ref, dos_ref, new_ref, traits_ref,
    residual_ref, scores_ref,
    x_ref, fresh_ref, st_src, st_dst, part, rs_dst, gath, gram_ref, w_ref,
    core_src, keep, core_dst, y_src, y_dst, rw_src, rw_dst, fin_src, fin_dst,
    st_s, st_r, rs_s, rs_r, ag_s, ag_r, fr_s, fr_r, core_s, core_r, y_s, y_r,
    rw_s, rw_r, fin_s, fin_r, tw_s, tw_r, tg_s, tg_r, tw_dst, rs_src, norm_ref,
):
    s = lax.axis_index("samp")
    b = lax.axis_index("blk")
    ny = nb // 2
    core = lax.rem(b, 2)
    y = b // 2
    rows, vb = dos_ref.shape
    nc = new_ref.shape[1]
    nt = traits_ref.shape[0]
    vblocks = vb // LANES
    own = RIDGE * share
    q = nb * own // ns
    k = ns // nb

    barrier = pltpu.get_barrier_semaphore()

    others = [(lax.rem(s + o, ns), b) for o in range(1, ns)]
    others += [(s, lax.rem(b + o, nb)) for o in range(1, nb)]
    for other in others:
        pl.semaphore_signal(barrier, inc=1, device_id=other, device_id_type=MESH)

    sends = []

    def send(src, dst, ssem, rsem, device):
        copy = pltpu.make_async_remote_copy(
            src_ref=src, dst_ref=dst, send_sem=ssem, recv_sem=rsem,
            device_id=device, device_id_type=MESH,
        )
        copy.start()
        sends.append(copy)
        return copy

    codes = dos_ref[...].astype(F32)
    st_src[0:1, :vb] = jnp.sum(codes, axis=0, keepdims=True)
    st_src[1:2, :vb] = jnp.sum(codes * codes, axis=0, keepdims=True)
    codes = new_ref[...].astype(F32)
    st_src[0:1, vb:] = jnp.sum(codes, axis=0, keepdims=True)
    st_src[1:2, vb:] = jnp.sum(codes * codes, axis=0, keepdims=True)

    pl.semaphore_wait(barrier, len(others))
    copies = []
    for o in range(1, ns):
        copies.append(
            send(st_src, st_dst.at[o], st_s.at[o], st_r.at[o], (lax.rem(s + o, ns), b))
        )
    stat = st_src[...]
    for o in range(1, ns):
        copies[o - 1].wait_recv()
        stat = stat + st_dst[o]
    mean = stat[0:1] / count
    inv = 1.0 / jnp.sqrt(stat[1:2] / count - mean * mean + 1e-05)
    fresh_ref[b] = ((new_ref[...].astype(F32) - mean[:, vb:]) * inv[:, vb:]).astype(BF16)
    fresh_copies = []
    for o in range(1, nb):
        fresh_copies.append(
            send(fresh_ref.at[b], fresh_ref.at[b], fr_s.at[o], fr_r.at[o], (s, lax.rem(b + o, nb)))
        )
    x_ref[...] = ((dos_ref[...].astype(F32) - mean[:, :vb]) * inv[:, :vb]).astype(BF16)

    x = x_ref[...]
    at = 0
    for i in range(vblocks):
        line = lax.dot_general(
            x[:, i * LANES : (i + 1) * LANES], x[:, i * LANES :],
            (((0,), (0,)), ((), ())), preferred_element_type=F32,
        ).astype(BF16)
        for j in range(vblocks - i):
            part[at : at + LANES, :] = line[:, j * LANES : (j + 1) * LANES]
            at += LANES
    cross = jnp.dot(
        traits_ref[...].astype(BF16), x, preferred_element_type=F32
    ).astype(BF16)
    for j in range(vblocks):
        part[at : at + nt, :] = cross[:, j * LANES : (j + 1) * LANES]
        at += nt
    if at < ns * chunk:
        part[at:, :] = jnp.zeros((ns * chunk - at, LANES), BF16)

    def piece(index):
        return pl.ds(pl.multiple_of(index * chunk, 16), chunk)

    np = ns // 2
    lane = lax.rem(s, 2)
    pair = s // 2
    twin = s + 1 - 2 * lane
    copies = []
    for o in list(range(1, np)) + [0]:
        to = 2 * lax.rem(pair + o, np) + 1 - lane
        copies.append(
            send(part.at[piece(to)], tw_dst.at[o], tw_s.at[o], tw_r.at[o], (twin, b))
        )
    arrivals = []
    for o in range(1, np):
        to = 2 * lax.rem(pair + o, np) + lane
        copies[o - 1].wait_recv()
        rs_src[o] = (part[piece(to), :].astype(F32) + tw_dst[o].astype(F32)).astype(BF16)
        arrivals.append(
            send(rs_src.at[o], rs_dst.at[o], rs_s.at[o], rs_r.at[o], (to, b))
        )
    copies[np - 1].wait_recv()
    summed = part[piece(s), :].astype(F32) + tw_dst[0].astype(F32)
    for o in range(1, np):
        arrivals[o - 1].wait_recv()
        summed = summed + rs_dst[o].astype(F32)
    gath[piece(s), :] = summed.astype(BF16)
    for o in range(1, np):
        to = 2 * lax.rem(pair + o, np) + lane
        send(gath.at[piece(s)], gath.at[piece(s)], ag_s.at[o], ag_r.at[o], (to, b))
    send(gath.at[piece(s)], gath.at[piece(s)], tg_s.at[0], tg_r.at[0], (twin, b))
    for o in range(1, np):
        source = 2 * lax.rem(pair - o + np, np) + lane
        pltpu.make_async_remote_copy(
            src_ref=gath.at[piece(source)], dst_ref=gath.at[piece(source)],
            send_sem=ag_s.at[o], recv_sem=ag_r.at[o],
            device_id=(source, b), device_id_type=MESH,
        ).wait_recv()
        send(gath.at[piece(source)], gath.at[piece(source)], tg_s.at[o], tg_r.at[o], (twin, b))
    for o in range(np):
        source = 2 * lax.rem(pair - o + np, np) + 1 - lane
        pltpu.make_async_remote_copy(
            src_ref=gath.at[piece(source)], dst_ref=gath.at[piece(source)],
            send_sem=tg_s.at[o], recv_sem=tg_r.at[o],
            device_id=(twin, b), device_id_type=MESH,
        ).wait_recv()

    at = 0
    for i in range(vblocks):
        for j in range(i, vblocks):
            block = gath[at : at + LANES, :].astype(F32)
            at += LANES
            gram_ref[i * LANES : (i + 1) * LANES, j * LANES : (j + 1) * LANES] = block.astype(BF16)
            if j > i:
                gram_ref[j * LANES : (j + 1) * LANES, i * LANES : (i + 1) * LANES] = block.T.astype(BF16)
    cross = jnp.concatenate(
        [gath[at + j * nt : at + (j + 1) * nt, :] for j in range(vblocks)], axis=1
    )
    gram = gram_ref[...]
    bound = jnp.max(
        jnp.sum(jnp.abs(gram.astype(F32)), axis=0, keepdims=True), axis=1, keepdims=True
    ) / count
    bound = jnp.broadcast_to(bound, (1, vb))

    def apply(value):
        high = value.astype(BF16)
        low = (value - high.astype(F32)).astype(BF16)
        return (
            jnp.dot(high, gram, preferred_element_type=F32)
            + jnp.dot(low, gram, preferred_element_type=F32)
        ) / count

    powers = [cross.astype(F32) / count]
    for _ in range(CHEB - 1):
        powers.append(apply(powers[-1]))
    for r in range(RIDGE):
        coefs = coefficients(jnp.full((1, vb), shrink_ref[r], F32), bound)
        weight = coefs[0] * powers[0]
        for c, v in zip(coefs[1:], powers[1:]):
            weight = weight + c * v
        weight = weight.astype(BF16)
        for d in range(nb):
            w_ref[d, r * share : (r + 1) * share, :] = weight[d * share : (d + 1) * share, :]

    for d in range(nb):
        pred = lax.dot_general(
            w_ref[d], x, (((1,), (1,)), ((), ())), preferred_element_type=F32
        )

        @pl.when(core == d % 2)
        def _():
            keep[d // 2] = pred

        @pl.when(core != d % 2)
        def _():
            core_src[d // 2] = pred.astype(BF16)

    copy = send(core_src, core_dst, core_s.at[0], core_r.at[0], (s, 2 * y + 1 - core))
    copy.wait_recv()
    copies = []
    for o in range(1, ny):
        to = lax.rem(y + o, ny)
        y_src[o] = (keep[to] + core_dst[to].astype(F32)).astype(BF16)
        copies.append(
            send(y_src.at[o], y_dst.at[o], y_s.at[o], y_r.at[o], (s, 2 * to + core))
        )
    pred = keep[y] + core_dst[y].astype(F32)
    for o in range(1, ny):
        copies[o - 1].wait_recv()
        pred = pred + y_dst[o].astype(F32)
    mine = traits_ref[pl.ds(pl.multiple_of(b * share, 8), share), :]
    resid = jnp.concatenate([mine] * RIDGE, axis=0) - pred
    for r in range(RIDGE):
        residual_ref[r] = resid[r * share : (r + 1) * share, :]
    res_bf = resid.astype(BF16)
    res_f = res_bf.astype(F32)
    squares = jnp.zeros((own, LANES), F32)
    for j in range(rows // LANES):
        v = res_f[:, j * LANES : (j + 1) * LANES]
        squares = squares + v * v
    wide = jnp.concatenate([squares, jnp.zeros((LANES - own, LANES), F32)], axis=0)
    sums = jnp.broadcast_to(jnp.sum(wide.T, axis=0, keepdims=True), (8, LANES))
    for copy in fresh_copies:
        copy.wait_recv()
    for d in range(nb):
        raw = jnp.dot(res_bf, fresh_ref[d], preferred_element_type=F32)
        for i in range(k):
            rw_src[d * k + i, :q, :] = raw[i * q : (i + 1) * q, :]
            rw_src[d * k + i, q:, :] = sums
    copies = []
    for o in range(1, ns):
        to = lax.rem(s + o, ns)
        copies.append(send(rw_src.at[to], rw_dst.at[o], rw_s.at[o], rw_r.at[o], (to, b)))
    raw = rw_src[s]
    for o in range(1, ns):
        copies[o - 1].wait_recv()
        raw = raw + rw_dst[o]

    goal = s // k
    slot = lax.rem(s, k)
    norm_ref[...] = raw[q:, :].T[:own, :]
    norm = norm_ref[pl.ds(pl.multiple_of(slot * q, 8), q), 0:1]
    score = raw[:q, :] / jnp.sqrt(count * (norm / count + 1e-05))
    extra = up(q, 16) - q
    if extra:
        score = jnp.concatenate([score, jnp.zeros((extra, nc), F32)], axis=0)
    fin_src[...] = score.astype(BF16)
    for o in range(ns):
        copy = pltpu.make_async_remote_copy(
            src_ref=fin_src, dst_ref=fin_dst.at[b, slot],
            send_sem=fin_s.at[o], recv_sem=fin_r.at[slot * nb + b],
            device_id=(lax.rem(s + o, ns), goal), device_id_type=MESH,
        )
        if o == 0:
            @pl.when(goal != b)
            def _():
                copy.start()

            @pl.when(goal == b)
            def _():
                fin_dst[b, slot] = fin_src[...]
        else:
            copy.start()
            sends.append(copy)
    for i in range(k):
        for d in range(nb):
            source = b * k + i

            @pl.when(jnp.logical_or(source != s, b != d))
            def _():
                pltpu.make_async_remote_copy(
                    src_ref=fin_src, dst_ref=fin_dst.at[d, i],
                    send_sem=fin_s.at[0], recv_sem=fin_r.at[i * nb + d],
                    device_id=(source, d), device_id_type=MESH,
                ).wait_recv()

    for d in range(nb):
        block = jnp.concatenate([fin_dst[d, i].astype(F32)[:q] for i in range(k)], axis=0)
        for r in range(RIDGE):
            scores_ref[r, d * share : (d + 1) * share, :] = block[r * share : (r + 1) * share, :]

    for copy in sends:
        copy.wait_send()

    @pl.when(goal != b)
    def _():
        pltpu.make_async_remote_copy(
            src_ref=fin_src, dst_ref=fin_dst.at[b, slot],
            send_sem=fin_s.at[0], recv_sem=fin_r.at[slot * nb + b],
            device_id=(s, goal), device_id_type=MESH,
        ).wait_send()


def shards(ns, nb, dosages, new_dosages, traits, shrink):
    rows, vb = dosages.shape
    nc = new_dosages.shape[1]
    real = traits.shape[0] // nb
    share = up(real, 16)
    if share != real:
        traits = jnp.pad(
            traits.reshape(nb, real, rows), ((0, 0), (0, share - real), (0, 0))
        ).reshape(nb * share, rows)
    nt = nb * share
    vblocks = vb // LANES
    chunk = up(-(-(vblocks * (vblocks + 1) // 2 * LANES + vblocks * nt) // ns), 16)
    own = RIDGE * share
    ny = nb // 2
    k = ns // nb
    q = own // k
    count = float(rows * ns)
    dma = pltpu.SemaphoreType.DMA
    vmem = pl.BlockSpec(memory_space=pltpu.VMEM)
    residual, scores = pl.pallas_call(
        functools.partial(kernel, ns, nb, share, count, chunk),
        out_shape=(
            jax.ShapeDtypeStruct((RIDGE, share, rows), F32),
            jax.ShapeDtypeStruct((RIDGE, nt, nc), F32),
        ),
        in_specs=[pl.BlockSpec(memory_space=pltpu.SMEM), vmem, vmem, vmem],
        out_specs=(vmem, vmem),
        scratch_shapes=[
            pltpu.VMEM((rows, vb), BF16),
            pltpu.VMEM((nb, rows, nc), BF16),
            pltpu.VMEM((2, vb + nc), F32),
            pltpu.VMEM((ns, 2, vb + nc), F32),
            pltpu.VMEM((ns * chunk, LANES), BF16),
            pltpu.VMEM((ns // 2, chunk, LANES), BF16),
            pltpu.VMEM((ns * chunk, LANES), BF16),
            pltpu.VMEM((vb, vb), BF16),
            pltpu.VMEM((nb, own, vb), BF16),
            pltpu.VMEM((ny, own, rows), BF16),
            pltpu.VMEM((ny, own, rows), F32),
            pltpu.VMEM((ny, own, rows), BF16),
            pltpu.VMEM((ny, own, rows), BF16),
            pltpu.VMEM((ny, own, rows), BF16),
            pltpu.VMEM((ns, q + 8, nc), F32),
            pltpu.VMEM((ns, q + 8, nc), F32),
            pltpu.VMEM((up(q, 16), nc), BF16),
            pltpu.VMEM((nb, k, up(q, 16), nc), BF16),
            dma((ns,)), dma((ns,)), dma((ns,)), dma((ns,)), dma((ns,)), dma((ns,)),
            dma((nb,)), dma((nb,)), dma((1,)), dma((1,)), dma((ny,)), dma((ny,)),
            dma((ns,)), dma((ns,)), dma((ns,)), dma((ns,)),
            dma((ns // 2,)), dma((ns // 2,)), dma((ns // 2,)), dma((ns // 2,)),
            pltpu.VMEM((ns // 2, chunk, LANES), BF16),
            pltpu.VMEM((ns // 2, chunk, LANES), BF16),
            pltpu.VMEM((own, 8), F32),
        ],
        compiler_params=pltpu.CompilerParams(
            collective_id=0, has_side_effects=True, vmem_limit_bytes=56 * 1024 * 1024
        ),
    )(shrink, dosages, new_dosages, traits)
    if share != real:
        residual = residual[:, :real]
        scores = scores.reshape(RIDGE, nb, share, nc)[:, :, :real].reshape(RIDGE, nb * real, nc)
    return residual, scores


def solution(mesh):
    placed = (P("samp", "blk"), P("samp", "blk"), P(None, "samp"), P())
    return jax.shard_map(
        functools.partial(shards, mesh.shape["samp"], mesh.shape["blk"]),
        mesh=mesh,
        in_specs=placed,
        out_specs=(P(None, "blk", "samp"), P(None, None, "blk")),
        check_vma=False,
    )
```

```python
import functools

import jax
import jax.numpy as jnp
from jax import lax
from jax.experimental import pallas as pl
from jax.experimental.pallas import tpu as pltpu
from jax.sharding import PartitionSpec as P

RIDGE = 5
CHEB = 3
LANES = 128
F32 = jnp.float32
BF16 = jnp.bfloat16
MESH = pl.DeviceIdType.MESH


def up(value, unit):
    return -(-value // unit) * unit


def coefficients(lam, bound):
    centre = lam + bound / 2.0
    half = bound / 2.0
    sig = centre / half
    factor = 1.0 / sig
    zero = jnp.zeros_like(centre)
    direction = [1.0 / centre] + [zero] * (CHEB - 1)
    remain = [zero + 1.0] + [zero] * (CHEB - 1)
    iterate = [zero] * CHEB
    for sweep in range(CHEB):
        iterate = [a + b for a, b in zip(iterate, direction)]
        if sweep + 1 < CHEB:
            applied = [lam * direction[0]] + [
                lam * direction[i] + direction[i - 1] for i in range(1, CHEB)
            ]
            remain = [a - b for a, b in zip(remain, applied)]
            following = 1.0 / (2.0 * sig - factor)
            direction = [
                following * factor * a + 2.0 * following / half * b
                for a, b in zip(direction, remain)
            ]
            factor = following
    return iterate


def kernel(
    ns, nb, share, count, chunk,
    shrink_ref, dos_ref, new_ref, traits_ref,
    residual_ref, scores_ref,
    x_ref, fresh_ref, st_src, st_dst, part, rs_dst, gath, gram_ref, w_ref,
    core_src, core_dst, y_src, y_dst, rw_src, rw_dst, fin_src, fin_dst,
    st_s, st_r, rs_s, rs_r, ag_s, ag_r, fr_s, fr_r, core_s, core_r, y_s, y_r,
    rw_s, rw_r, fin_s, fin_r, tw_s, tw_r, tg_s, tg_r, tw_dst, rs_src, norm_ref, st_sum, fc_s, fc_r,
):
    s = lax.axis_index("samp")
    b = lax.axis_index("blk")
    ny = nb // 2
    core = lax.rem(b, 2)
    y = b // 2
    rows, vb = dos_ref.shape
    nc = new_ref.shape[1]
    nt = traits_ref.shape[0]
    vblocks = vb // LANES
    own = RIDGE * share
    q = nb * own // ns
    k = ns // nb

    barrier = pltpu.get_barrier_semaphore()

    np = ns // 2
    lane = lax.rem(s, 2)
    pair = s // 2
    twin = s + 1 - 2 * lane
    sibling = 2 * y + 1 - core
    others = [(twin, b), (s, sibling)]
    others += [(2 * lax.rem(pair + o, np) + lane, b) for o in range(1, np)]
    others += [(s, 2 * lax.rem(y + o, ny) + core) for o in range(1, ny)]
    for other in others:
        pl.semaphore_signal(barrier, inc=1, device_id=other, device_id_type=MESH)

    sends = []

    def send(src, dst, ssem, rsem, device):
        copy = pltpu.make_async_remote_copy(
            src_ref=src, dst_ref=dst, send_sem=ssem, recv_sem=rsem,
            device_id=device, device_id_type=MESH,
        )
        copy.start()
        sends.append(copy)
        return copy

    codes = dos_ref[...].astype(F32)
    st_src[0:1, :vb] = jnp.sum(codes, axis=0, keepdims=True)
    st_src[1:2, :vb] = jnp.sum(codes * codes, axis=0, keepdims=True)
    codes = new_ref[...].astype(F32)
    st_src[0:1, vb:] = jnp.sum(codes, axis=0, keepdims=True)
    st_src[1:2, vb:] = jnp.sum(codes * codes, axis=0, keepdims=True)

    pl.semaphore_wait(barrier, len(others))
    send(st_src, st_dst.at[0], st_s.at[0], st_r.at[0], (twin, b)).wait_recv()
    st_sum[...] = st_src[...] + st_dst[0]
    copies = []
    for o in range(1, np):
        to = 2 * lax.rem(pair + o, np) + lane
        copies.append(send(st_sum, st_dst.at[o], st_s.at[o], st_r.at[o], (to, b)))
    stat = st_sum[...]
    for copy, o in zip(copies, range(1, np)):
        copy.wait_recv()
        stat = stat + st_dst[o]
    mean = stat[0:1] / count
    inv = 1.0 / jnp.sqrt(stat[1:2] / count - mean * mean + 1e-05)
    fresh_ref[b] = ((new_ref[...].astype(F32) - mean[:, vb:]) * inv[:, vb:]).astype(BF16)
    for o in range(1, ny):
        to = 2 * lax.rem(y + o, ny) + core
        send(fresh_ref.at[b], fresh_ref.at[b], fr_s.at[o], fr_r.at[o], (s, to))
    send(fresh_ref.at[b], fresh_ref.at[b], fc_s.at[0], fc_r.at[0], (s, sibling))
    x_ref[...] = ((dos_ref[...].astype(F32) - mean[:, :vb]) * inv[:, :vb]).astype(BF16)

    x = x_ref[...]
    at = 0
    for i in range(vblocks):
        line = lax.dot_general(
            x[:, i * LANES : (i + 1) * LANES], x[:, i * LANES :],
            (((0,), (0,)), ((), ())), preferred_element_type=F32,
        ).astype(BF16)
        for j in range(vblocks - i):
            part[at : at + LANES, :] = line[:, j * LANES : (j + 1) * LANES]
            at += LANES
    cross = jnp.dot(
        traits_ref[...].astype(BF16), x, preferred_element_type=F32
    ).astype(BF16)
    for j in range(vblocks):
        part[at : at + nt, :] = cross[:, j * LANES : (j + 1) * LANES]
        at += nt
    if at < ns * chunk:
        part[at:, :] = jnp.zeros((ns * chunk - at, LANES), BF16)

    def piece(index):
        return pl.ds(pl.multiple_of(index * chunk, 16), chunk)

    copies = []
    for o in list(range(1, np)) + [0]:
        to = 2 * lax.rem(pair + o, np) + 1 - lane
        copies.append(
            send(part.at[piece(to)], tw_dst.at[o], tw_s.at[o], tw_r.at[o], (twin, b))
        )
    arrivals = []
    for o in range(1, np):
        to = 2 * lax.rem(pair + o, np) + lane
        copies[o - 1].wait_recv()
        rs_src[o] = (part[piece(to), :].astype(F32) + tw_dst[o].astype(F32)).astype(BF16)
        arrivals.append(
            send(rs_src.at[o], rs_dst.at[o], rs_s.at[o], rs_r.at[o], (to, b))
        )
    copies[np - 1].wait_recv()
    summed = part[piece(s), :].astype(F32) + tw_dst[0].astype(F32)
    for o in range(1, np):
        arrivals[o - 1].wait_recv()
        summed = summed + rs_dst[o].astype(F32)
    gath[piece(s), :] = summed.astype(BF16)
    for o in range(1, np):
        to = 2 * lax.rem(pair + o, np) + lane
        send(gath.at[piece(s)], gath.at[piece(s)], ag_s.at[o], ag_r.at[o], (to, b))
    send(gath.at[piece(s)], gath.at[piece(s)], tg_s.at[0], tg_r.at[0], (twin, b))
    for o in range(1, np):
        source = 2 * lax.rem(pair - o + np, np) + lane
        pltpu.make_async_remote_copy(
            src_ref=gath.at[piece(source)], dst_ref=gath.at[piece(source)],
            send_sem=ag_s.at[o], recv_sem=ag_r.at[o],
            device_id=(source, b), device_id_type=MESH,
        ).wait_recv()
        send(gath.at[piece(source)], gath.at[piece(source)], tg_s.at[o], tg_r.at[o], (twin, b))
    for o in range(np):
        source = 2 * lax.rem(pair - o + np, np) + 1 - lane
        pltpu.make_async_remote_copy(
            src_ref=gath.at[piece(source)], dst_ref=gath.at[piece(source)],
            send_sem=tg_s.at[o], recv_sem=tg_r.at[o],
            device_id=(twin, b), device_id_type=MESH,
        ).wait_recv()

    at = 0
    for i in range(vblocks):
        for j in range(i, vblocks):
            block = gath[at : at + LANES, :].astype(F32)
            at += LANES
            gram_ref[i * LANES : (i + 1) * LANES, j * LANES : (j + 1) * LANES] = block.astype(BF16)
            if j > i:
                gram_ref[j * LANES : (j + 1) * LANES, i * LANES : (i + 1) * LANES] = block.T.astype(BF16)
    cross = jnp.concatenate(
        [gath[at + j * nt : at + (j + 1) * nt, :] for j in range(vblocks)], axis=1
    )
    gram = gram_ref[...]
    bound = jnp.max(
        jnp.sum(jnp.abs(gram.astype(F32)), axis=0, keepdims=True), axis=1, keepdims=True
    ) / count
    bound = jnp.broadcast_to(bound, (1, vb))

    def apply(value):
        high = value.astype(BF16)
        low = (value - high.astype(F32)).astype(BF16)
        return (
            jnp.dot(high, gram, preferred_element_type=F32)
            + jnp.dot(low, gram, preferred_element_type=F32)
        ) / count

    powers = [cross.astype(F32) / count]
    for _ in range(CHEB - 1):
        powers.append(apply(powers[-1]))
    for r in range(RIDGE):
        coefs = coefficients(jnp.full((1, vb), shrink_ref[r], F32), bound)
        weight = coefs[0] * powers[0]
        for c, v in zip(coefs[1:], powers[1:]):
            weight = weight + c * v
        weight = weight.astype(BF16)
        for d in range(nb):
            w_ref[d, r * share : (r + 1) * share, :] = weight[d * share : (d + 1) * share, :]

    def predict(d):
        return lax.dot_general(
            w_ref[d], x, (((1,), (1,)), ((), ())), preferred_element_type=F32
        )

    copies = []
    for o in list(range(1, ny)) + [0]:
        to = lax.rem(y + o, ny)
        core_src[o] = predict(2 * to + 1 - core).astype(BF16)
        copy = send(core_src.at[o], core_dst.at[o], core_s.at[o], core_r.at[o], (s, sibling))
        pred = predict(2 * to + core)
        copy.wait_recv()
        pred = pred + core_dst[o].astype(F32)
        if o:
            y_src[o] = pred.astype(BF16)
            copies.append(
                send(y_src.at[o], y_dst.at[o], y_s.at[o], y_r.at[o], (s, 2 * to + core))
            )
    for o in range(1, ny):
        source = 2 * lax.rem(y - o + ny, ny) + core
        pltpu.make_async_remote_copy(
            src_ref=fresh_ref.at[source], dst_ref=fresh_ref.at[source],
            send_sem=fr_s.at[o], recv_sem=fr_r.at[o],
            device_id=(s, source), device_id_type=MESH,
        ).wait_recv()
        send(fresh_ref.at[source], fresh_ref.at[source], fc_s.at[o], fc_r.at[o], (s, sibling))
    for o in range(1, ny):
        copies[o - 1].wait_recv()
        pred = pred + y_dst[o].astype(F32)
    mine = traits_ref[pl.ds(pl.multiple_of(b * share, 8), share), :]
    resid = jnp.concatenate([mine] * RIDGE, axis=0) - pred
    for r in range(RIDGE):
        residual_ref[r] = resid[r * share : (r + 1) * share, :]
    res_bf = resid.astype(BF16)
    res_f = res_bf.astype(F32)
    squares = jnp.zeros((own, LANES), F32)
    for j in range(rows // LANES):
        v = res_f[:, j * LANES : (j + 1) * LANES]
        squares = squares + v * v
    wide = jnp.concatenate([squares, jnp.zeros((LANES - own, LANES), F32)], axis=0)
    sums = jnp.broadcast_to(jnp.sum(wide.T, axis=0, keepdims=True), (8, LANES))
    for o in range(ny):
        source = 2 * lax.rem(y - o + ny, ny) + 1 - core
        pltpu.make_async_remote_copy(
            src_ref=fresh_ref.at[source], dst_ref=fresh_ref.at[source],
            send_sem=fc_s.at[o], recv_sem=fc_r.at[o],
            device_id=(s, sibling), device_id_type=MESH,
        ).wait_recv()
    for d in range(nb):
        raw = jnp.dot(res_bf, fresh_ref[d], preferred_element_type=F32)
        for i in range(k):
            rw_src[d * k + i, :q, :] = raw[i * q : (i + 1) * q, :]
            rw_src[d * k + i, q:, :] = sums
    copies = []
    for o in range(1, ns):
        to = lax.rem(s + o, ns)
        copies.append(send(rw_src.at[to], rw_dst.at[o], rw_s.at[o], rw_r.at[o], (to, b)))
    raw = rw_src[s]
    for o in range(1, ns):
        copies[o - 1].wait_recv()
        raw = raw + rw_dst[o]

    goal = s // k
    slot = lax.rem(s, k)
    norm_ref[...] = raw[q:, :].T[:own, :]
    norm = norm_ref[pl.ds(pl.multiple_of(slot * q, 8), q), 0:1]
    score = raw[:q, :] / jnp.sqrt(count * (norm / count + 1e-05))
    extra = up(q, 16) - q
    if extra:
        score = jnp.concatenate([score, jnp.zeros((extra, nc), F32)], axis=0)
    fin_src[...] = score.astype(BF16)
    for o in range(ns):
        copy = pltpu.make_async_remote_copy(
            src_ref=fin_src, dst_ref=fin_dst.at[b, slot],
            send_sem=fin_s.at[o], recv_sem=fin_r.at[slot * nb + b],
            device_id=(lax.rem(s + o, ns), goal), device_id_type=MESH,
        )
        if o == 0:
            @pl.when(goal != b)
            def _():
                copy.start()

            @pl.when(goal == b)
            def _():
                fin_dst[b, slot] = fin_src[...]
        else:
            copy.start()
            sends.append(copy)
    for i in range(k):
        for d in range(nb):
            source = b * k + i

            @pl.when(jnp.logical_or(source != s, b != d))
            def _():
                pltpu.make_async_remote_copy(
                    src_ref=fin_src, dst_ref=fin_dst.at[d, i],
                    send_sem=fin_s.at[0], recv_sem=fin_r.at[i * nb + d],
                    device_id=(source, d), device_id_type=MESH,
                ).wait_recv()

    for d in range(nb):
        block = jnp.concatenate([fin_dst[d, i].astype(F32)[:q] for i in range(k)], axis=0)
        for r in range(RIDGE):
            scores_ref[r, d * share : (d + 1) * share, :] = block[r * share : (r + 1) * share, :]

    for copy in sends:
        copy.wait_send()

    @pl.when(goal != b)
    def _():
        pltpu.make_async_remote_copy(
            src_ref=fin_src, dst_ref=fin_dst.at[b, slot],
            send_sem=fin_s.at[0], recv_sem=fin_r.at[slot * nb + b],
            device_id=(s, goal), device_id_type=MESH,
        ).wait_send()


def shards(ns, nb, dosages, new_dosages, traits, shrink):
    rows, vb = dosages.shape
    nc = new_dosages.shape[1]
    real = traits.shape[0] // nb
    share = up(real, 16)
    if share != real:
        traits = jnp.pad(
            traits.reshape(nb, real, rows), ((0, 0), (0, share - real), (0, 0))
        ).reshape(nb * share, rows)
    nt = nb * share
    vblocks = vb // LANES
    chunk = up(-(-(vblocks * (vblocks + 1) // 2 * LANES + vblocks * nt) // ns), 16)
    own = RIDGE * share
    ny = nb // 2
    k = ns // nb
    q = own // k
    count = float(rows * ns)
    dma = pltpu.SemaphoreType.DMA
    vmem = pl.BlockSpec(memory_space=pltpu.VMEM)
    residual, scores = pl.pallas_call(
        functools.partial(kernel, ns, nb, share, count, chunk),
        out_shape=(
            jax.ShapeDtypeStruct((RIDGE, share, rows), F32),
            jax.ShapeDtypeStruct((RIDGE, nt, nc), F32),
        ),
        in_specs=[pl.BlockSpec(memory_space=pltpu.SMEM), vmem, vmem, vmem],
        out_specs=(vmem, vmem),
        scratch_shapes=[
            pltpu.VMEM((rows, vb), BF16),
            pltpu.VMEM((nb, rows, nc), BF16),
            pltpu.VMEM((2, vb + nc), F32),
            pltpu.VMEM((ns, 2, vb + nc), F32),
            pltpu.VMEM((ns * chunk, LANES), BF16),
            pltpu.VMEM((ns // 2, chunk, LANES), BF16),
            pltpu.VMEM((ns * chunk, LANES), BF16),
            pltpu.VMEM((vb, vb), BF16),
            pltpu.VMEM((nb, own, vb), BF16),
            pltpu.VMEM((ny, own, rows), BF16),
            pltpu.VMEM((ny, own, rows), BF16),
            pltpu.VMEM((ny, own, rows), BF16),
            pltpu.VMEM((ny, own, rows), BF16),
            pltpu.VMEM((ns, q + 8, nc), F32),
            pltpu.VMEM((ns, q + 8, nc), F32),
            pltpu.VMEM((up(q, 16), nc), BF16),
            pltpu.VMEM((nb, k, up(q, 16), nc), BF16),
            dma((ns,)), dma((ns,)), dma((ns,)), dma((ns,)), dma((ns,)), dma((ns,)),
            dma((ny,)), dma((ny,)), dma((ny,)), dma((ny,)), dma((ny,)), dma((ny,)),
            dma((ns,)), dma((ns,)), dma((ns,)), dma((ns,)),
            dma((ns // 2,)), dma((ns // 2,)), dma((ns // 2,)), dma((ns // 2,)),
            pltpu.VMEM((ns // 2, chunk, LANES), BF16),
            pltpu.VMEM((ns // 2, chunk, LANES), BF16),
            pltpu.VMEM((own, 8), F32),
            pltpu.VMEM((2, vb + nc), F32),
            dma((ny,)), dma((ny,)),
        ],
        compiler_params=pltpu.CompilerParams(
            collective_id=0, has_side_effects=True, vmem_limit_bytes=56 * 1024 * 1024
        ),
    )(shrink, dosages, new_dosages, traits)
    if share != real:
        residual = residual[:, :real]
        scores = scores.reshape(RIDGE, nb, share, nc)[:, :, :real].reshape(RIDGE, nb * real, nc)
    return residual, scores


def solution(mesh):
    placed = (P("samp", "blk"), P("samp", "blk"), P(None, "samp"), P())
    return jax.shard_map(
        functools.partial(shards, mesh.shape["samp"], mesh.shape["blk"]),
        mesh=mesh,
        in_specs=placed,
        out_specs=(P(None, "blk", "samp"), P(None, None, "blk")),
        check_vma=False,
    )
```

```python
import functools

import jax
import jax.numpy as jnp
from jax import lax
from jax.experimental import pallas as pl
from jax.experimental.pallas import tpu as pltpu
from jax.sharding import PartitionSpec as P

RIDGE = 5
CHEB = 3
LANES = 128
F32 = jnp.float32
BF16 = jnp.bfloat16
MESH = pl.DeviceIdType.MESH


def up(value, unit):
    return -(-value // unit) * unit


def coefficients(lam, bound):
    centre = lam + bound / 2.0
    half = bound / 2.0
    sig = centre / half
    factor = 1.0 / sig
    zero = jnp.zeros_like(centre)
    direction = [1.0 / centre] + [zero] * (CHEB - 1)
    remain = [zero + 1.0] + [zero] * (CHEB - 1)
    iterate = [zero] * CHEB
    for sweep in range(CHEB):
        iterate = [a + b for a, b in zip(iterate, direction)]
        if sweep + 1 < CHEB:
            applied = [lam * direction[0]] + [
                lam * direction[i] + direction[i - 1] for i in range(1, CHEB)
            ]
            remain = [a - b for a, b in zip(remain, applied)]
            following = 1.0 / (2.0 * sig - factor)
            direction = [
                following * factor * a + 2.0 * following / half * b
                for a, b in zip(direction, remain)
            ]
            factor = following
    return iterate


def kernel(
    ns, nb, share, count, chunk,
    shrink_ref, dos_ref, new_ref, traits_ref,
    residual_ref, scores_ref,
    x_ref, fresh_ref, st_src, st_dst, part, rs_dst, gath, gram_ref, w_ref,
    core_src, core_dst, y_src, y_dst, rw_src, rw_dst, fin_src, fin_dst,
    st_s, st_r, rs_s, rs_r, ag_s, ag_r, fr_s, fr_r, core_s, core_r, y_s, y_r,
    rw_s, rw_r, fin_s, fin_r, tg_s, tg_r, norm_ref, fc_s, fc_r,
):
    s = lax.axis_index("samp")
    b = lax.axis_index("blk")
    ny = nb // 2
    core = lax.rem(b, 2)
    y = b // 2
    rows, vb = dos_ref.shape
    nc = new_ref.shape[1]
    nt = traits_ref.shape[0]
    vblocks = vb // LANES
    own = RIDGE * share
    q = nb * own // ns
    k = ns // nb

    barrier = pltpu.get_barrier_semaphore()

    np = ns // 2
    lane = lax.rem(s, 2)
    pair = s // 2
    twin = s + 1 - 2 * lane
    sibling = 2 * y + 1 - core
    others = [(lax.rem(s + o, ns), b) for o in range(1, ns)] + [(s, sibling)]
    others += [(s, 2 * lax.rem(y + o, ny) + core) for o in range(1, ny)]
    for other in others:
        pl.semaphore_signal(barrier, inc=1, device_id=other, device_id_type=MESH)

    sends = []

    def send(src, dst, ssem, rsem, device):
        copy = pltpu.make_async_remote_copy(
            src_ref=src, dst_ref=dst, send_sem=ssem, recv_sem=rsem,
            device_id=device, device_id_type=MESH,
        )
        copy.start()
        sends.append(copy)
        return copy

    codes = dos_ref[...].astype(F32)
    st_src[0:1, :vb] = jnp.sum(codes, axis=0, keepdims=True)
    st_src[1:2, :vb] = jnp.sum(codes * codes, axis=0, keepdims=True)
    codes = new_ref[...].astype(F32)
    st_src[0:1, vb:] = jnp.sum(codes, axis=0, keepdims=True)
    st_src[1:2, vb:] = jnp.sum(codes * codes, axis=0, keepdims=True)

    pl.semaphore_wait(barrier, len(others))
    copies = []
    for o in range(1, ns):
        copies.append(
            send(st_src, st_dst.at[o], st_s.at[o], st_r.at[o], (lax.rem(s + o, ns), b))
        )
    stat = st_src[...]
    for o in range(1, ns):
        copies[o - 1].wait_recv()
        stat = stat + st_dst[o]
    mean = stat[0:1] / count
    inv = 1.0 / jnp.sqrt(stat[1:2] / count - mean * mean + 1e-05)
    fresh_ref[b] = ((new_ref[...].astype(F32) - mean[:, vb:]) * inv[:, vb:]).astype(BF16)
    for o in range(1, ny):
        to = 2 * lax.rem(y + o, ny) + core
        send(fresh_ref.at[b], fresh_ref.at[b], fr_s.at[o], fr_r.at[o], (s, to))
    send(fresh_ref.at[b], fresh_ref.at[b], fc_s.at[0], fc_r.at[0], (s, sibling))
    x_ref[...] = ((dos_ref[...].astype(F32) - mean[:, :vb]) * inv[:, :vb]).astype(BF16)

    x = x_ref[...]
    at = 0
    for i in range(vblocks):
        line = lax.dot_general(
            x[:, i * LANES : (i + 1) * LANES], x[:, i * LANES :],
            (((0,), (0,)), ((), ())), preferred_element_type=F32,
        ).astype(BF16)
        for j in range(vblocks - i):
            part[at : at + LANES, :] = line[:, j * LANES : (j + 1) * LANES]
            at += LANES
    cross = jnp.dot(
        traits_ref[...].astype(BF16), x, preferred_element_type=F32
    ).astype(BF16)
    for j in range(vblocks):
        part[at : at + nt, :] = cross[:, j * LANES : (j + 1) * LANES]
        at += nt
    if at < ns * chunk:
        part[at:, :] = jnp.zeros((ns * chunk - at, LANES), BF16)

    def piece(index):
        return pl.ds(pl.multiple_of(index * chunk, 16), chunk)

    copies = []
    for o in range(1, ns):
        to = lax.rem(s + o, ns)
        copies.append(
            send(part.at[piece(to)], rs_dst.at[o], rs_s.at[o], rs_r.at[o], (to, b))
        )
    summed = part[piece(s), :].astype(F32)
    for o in range(1, ns):
        copies[o - 1].wait_recv()
        summed = summed + rs_dst[o].astype(F32)
    gath[piece(s), :] = summed.astype(BF16)
    for o in range(1, np):
        to = 2 * lax.rem(pair + o, np) + lane
        send(gath.at[piece(s)], gath.at[piece(s)], ag_s.at[o], ag_r.at[o], (to, b))
    send(gath.at[piece(s)], gath.at[piece(s)], tg_s.at[0], tg_r.at[0], (twin, b))
    for o in range(1, np):
        source = 2 * lax.rem(pair - o + np, np) + lane
        pltpu.make_async_remote_copy(
            src_ref=gath.at[piece(source)], dst_ref=gath.at[piece(source)],
            send_sem=ag_s.at[o], recv_sem=ag_r.at[o],
            device_id=(source, b), device_id_type=MESH,
        ).wait_recv()
        send(gath.at[piece(source)], gath.at[piece(source)], tg_s.at[o], tg_r.at[o], (twin, b))
    for o in range(np):
        source = 2 * lax.rem(pair - o + np, np) + 1 - lane
        pltpu.make_async_remote_copy(
            src_ref=gath.at[piece(source)], dst_ref=gath.at[piece(source)],
            send_sem=tg_s.at[o], recv_sem=tg_r.at[o],
            device_id=(twin, b), device_id_type=MESH,
        ).wait_recv()

    at = 0
    for i in range(vblocks):
        for j in range(i, vblocks):
            block = gath[at : at + LANES, :].astype(F32)
            at += LANES
            gram_ref[i * LANES : (i + 1) * LANES, j * LANES : (j + 1) * LANES] = block.astype(BF16)
            if j > i:
                gram_ref[j * LANES : (j + 1) * LANES, i * LANES : (i + 1) * LANES] = block.T.astype(BF16)
    cross = jnp.concatenate(
        [gath[at + j * nt : at + (j + 1) * nt, :] for j in range(vblocks)], axis=1
    )
    gram = gram_ref[...]
    bound = jnp.max(
        jnp.sum(jnp.abs(gram.astype(F32)), axis=0, keepdims=True), axis=1, keepdims=True
    ) / count
    bound = jnp.broadcast_to(bound, (1, vb))

    def apply(value):
        high = value.astype(BF16)
        low = (value - high.astype(F32)).astype(BF16)
        return (
            jnp.dot(high, gram, preferred_element_type=F32)
            + jnp.dot(low, gram, preferred_element_type=F32)
        ) / count

    powers = [cross.astype(F32) / count]
    for _ in range(CHEB - 1):
        powers.append(apply(powers[-1]))
    for r in range(RIDGE):
        coefs = coefficients(jnp.full((1, vb), shrink_ref[r], F32), bound)
        weight = coefs[0] * powers[0]
        for c, v in zip(coefs[1:], powers[1:]):
            weight = weight + c * v
        weight = weight.astype(BF16)
        for d in range(nb):
            w_ref[d, r * share : (r + 1) * share, :] = weight[d * share : (d + 1) * share, :]

    def predict(d):
        return lax.dot_general(
            w_ref[d], x, (((1,), (1,)), ((), ())), preferred_element_type=F32
        )

    copies = []
    for o in list(range(1, ny)) + [0]:
        to = lax.rem(y + o, ny)
        core_src[o] = predict(2 * to + 1 - core).astype(BF16)
        copy = send(core_src.at[o], core_dst.at[o], core_s.at[o], core_r.at[o], (s, sibling))
        pred = predict(2 * to + core)
        copy.wait_recv()
        pred = pred + core_dst[o].astype(F32)
        if o:
            y_src[o] = pred.astype(BF16)
            copies.append(
                send(y_src.at[o], y_dst.at[o], y_s.at[o], y_r.at[o], (s, 2 * to + core))
            )
    for o in range(1, ny):
        source = 2 * lax.rem(y - o + ny, ny) + core
        pltpu.make_async_remote_copy(
            src_ref=fresh_ref.at[source], dst_ref=fresh_ref.at[source],
            send_sem=fr_s.at[o], recv_sem=fr_r.at[o],
            device_id=(s, source), device_id_type=MESH,
        ).wait_recv()
        send(fresh_ref.at[source], fresh_ref.at[source], fc_s.at[o], fc_r.at[o], (s, sibling))
    for o in range(1, ny):
        copies[o - 1].wait_recv()
        pred = pred + y_dst[o].astype(F32)
    mine = traits_ref[pl.ds(pl.multiple_of(b * share, 8), share), :]
    resid = jnp.concatenate([mine] * RIDGE, axis=0) - pred
    for r in range(RIDGE):
        residual_ref[r] = resid[r * share : (r + 1) * share, :]
    res_bf = resid.astype(BF16)
    res_f = res_bf.astype(F32)
    squares = jnp.zeros((own, LANES), F32)
    for j in range(rows // LANES):
        v = res_f[:, j * LANES : (j + 1) * LANES]
        squares = squares + v * v
    wide = jnp.concatenate([squares, jnp.zeros((LANES - own, LANES), F32)], axis=0)
    sums = jnp.broadcast_to(jnp.sum(wide.T, axis=0, keepdims=True), (8, LANES))
    for o in range(ny):
        source = 2 * lax.rem(y - o + ny, ny) + 1 - core
        pltpu.make_async_remote_copy(
            src_ref=fresh_ref.at[source], dst_ref=fresh_ref.at[source],
            send_sem=fc_s.at[o], recv_sem=fc_r.at[o],
            device_id=(s, sibling), device_id_type=MESH,
        ).wait_recv()
    for d in range(nb):
        raw = jnp.dot(res_bf, fresh_ref[d], preferred_element_type=F32)
        for i in range(k):
            rw_src[d * k + i, :q, :] = raw[i * q : (i + 1) * q, :]
            rw_src[d * k + i, q:, :] = sums
    copies = []
    for o in range(1, ns):
        to = lax.rem(s + o, ns)
        copies.append(send(rw_src.at[to], rw_dst.at[o], rw_s.at[o], rw_r.at[o], (to, b)))
    raw = rw_src[s]
    for o in range(1, ns):
        copies[o - 1].wait_recv()
        raw = raw + rw_dst[o]

    goal = s // k
    slot = lax.rem(s, k)
    norm_ref[...] = raw[q:, :].T[:own, :]
    norm = norm_ref[pl.ds(pl.multiple_of(slot * q, 8), q), 0:1]
    score = raw[:q, :] / jnp.sqrt(count * (norm / count + 1e-05))
    extra = up(q, 16) - q
    if extra:
        score = jnp.concatenate([score, jnp.zeros((extra, nc), F32)], axis=0)
    fin_src[...] = score.astype(BF16)
    for o in range(ns):
        copy = pltpu.make_async_remote_copy(
            src_ref=fin_src, dst_ref=fin_dst.at[b, slot],
            send_sem=fin_s.at[o], recv_sem=fin_r.at[slot * nb + b],
            device_id=(lax.rem(s + o, ns), goal), device_id_type=MESH,
        )
        if o == 0:
            @pl.when(goal != b)
            def _():
                copy.start()

            @pl.when(goal == b)
            def _():
                fin_dst[b, slot] = fin_src[...]
        else:
            copy.start()
            sends.append(copy)
    for i in range(k):
        for d in range(nb):
            source = b * k + i

            @pl.when(jnp.logical_or(source != s, b != d))
            def _():
                pltpu.make_async_remote_copy(
                    src_ref=fin_src, dst_ref=fin_dst.at[d, i],
                    send_sem=fin_s.at[0], recv_sem=fin_r.at[i * nb + d],
                    device_id=(source, d), device_id_type=MESH,
                ).wait_recv()

    for d in range(nb):
        block = jnp.concatenate([fin_dst[d, i].astype(F32)[:q] for i in range(k)], axis=0)
        for r in range(RIDGE):
            scores_ref[r, d * share : (d + 1) * share, :] = block[r * share : (r + 1) * share, :]

    for copy in sends:
        copy.wait_send()

    @pl.when(goal != b)
    def _():
        pltpu.make_async_remote_copy(
            src_ref=fin_src, dst_ref=fin_dst.at[b, slot],
            send_sem=fin_s.at[0], recv_sem=fin_r.at[slot * nb + b],
            device_id=(s, goal), device_id_type=MESH,
        ).wait_send()


def shards(ns, nb, dosages, new_dosages, traits, shrink):
    rows, vb = dosages.shape
    nc = new_dosages.shape[1]
    real = traits.shape[0] // nb
    share = up(real, 16)
    if share != real:
        traits = jnp.pad(
            traits.reshape(nb, real, rows), ((0, 0), (0, share - real), (0, 0))
        ).reshape(nb * share, rows)
    nt = nb * share
    vblocks = vb // LANES
    chunk = up(-(-(vblocks * (vblocks + 1) // 2 * LANES + vblocks * nt) // ns), 16)
    own = RIDGE * share
    ny = nb // 2
    k = ns // nb
    q = own // k
    count = float(rows * ns)
    dma = pltpu.SemaphoreType.DMA
    vmem = pl.BlockSpec(memory_space=pltpu.VMEM)
    residual, scores = pl.pallas_call(
        functools.partial(kernel, ns, nb, share, count, chunk),
        out_shape=(
            jax.ShapeDtypeStruct((RIDGE, share, rows), F32),
            jax.ShapeDtypeStruct((RIDGE, nt, nc), F32),
        ),
        in_specs=[pl.BlockSpec(memory_space=pltpu.SMEM), vmem, vmem, vmem],
        out_specs=(vmem, vmem),
        scratch_shapes=[
            pltpu.VMEM((rows, vb), BF16),
            pltpu.VMEM((nb, rows, nc), BF16),
            pltpu.VMEM((2, vb + nc), F32),
            pltpu.VMEM((ns, 2, vb + nc), F32),
            pltpu.VMEM((ns * chunk, LANES), BF16),
            pltpu.VMEM((ns, chunk, LANES), BF16),
            pltpu.VMEM((ns * chunk, LANES), BF16),
            pltpu.VMEM((vb, vb), BF16),
            pltpu.VMEM((nb, own, vb), BF16),
            pltpu.VMEM((ny, own, rows), BF16),
            pltpu.VMEM((ny, own, rows), BF16),
            pltpu.VMEM((ny, own, rows), BF16),
            pltpu.VMEM((ny, own, rows), BF16),
            pltpu.VMEM((ns, q + 8, nc), F32),
            pltpu.VMEM((ns, q + 8, nc), F32),
            pltpu.VMEM((up(q, 16), nc), BF16),
            pltpu.VMEM((nb, k, up(q, 16), nc), BF16),
            dma((ns,)), dma((ns,)), dma((ns,)), dma((ns,)), dma((ns,)), dma((ns,)),
            dma((ny,)), dma((ny,)), dma((ny,)), dma((ny,)), dma((ny,)), dma((ny,)),
            dma((ns,)), dma((ns,)), dma((ns,)), dma((ns,)),
            dma((ns // 2,)), dma((ns // 2,)),
            pltpu.VMEM((own, 8), F32),
            dma((ny,)), dma((ny,)),
        ],
        compiler_params=pltpu.CompilerParams(
            collective_id=0, has_side_effects=True, vmem_limit_bytes=56 * 1024 * 1024
        ),
    )(shrink, dosages, new_dosages, traits)
    if share != real:
        residual = residual[:, :real]
        scores = scores.reshape(RIDGE, nb, share, nc)[:, :, :real].reshape(RIDGE, nb * real, nc)
    return residual, scores


def solution(mesh):
    placed = (P("samp", "blk"), P("samp", "blk"), P(None, "samp"), P())
    return jax.shard_map(
        functools.partial(shards, mesh.shape["samp"], mesh.shape["blk"]),
        mesh=mesh,
        in_specs=placed,
        out_specs=(P(None, "blk", "samp"), P(None, None, "blk")),
        check_vma=False,
    )
```
